32 devices in a mesh: seq: 8 (over z, core), tp: 4 (over y, x).
Axes of the slice: x: 2, y: 2, z: 4, core: 2. Of those that a mesh axis runs over, the one named last changes fastest.
Arguments:
- queries: bfloat16 [512, 8192], P(None, 'tp'), may hold values from -80 to 80
- cache: bfloat16 [2, 8, 8192, 1024], P(None, None, 'seq', 'tp'), may hold values from -6 to 6
- draft_kv: bfloat16 [2, 512, 1024], P(None, 'seq', 'tp'), may hold values from -9 to 9
- out_weight: bfloat16 [8192, 8192], P('tp', 'seq'), may hold values from -0.0625 to 0.0625
- lengths: int32 [8], replicated, may hold values from 508 to 8184, as said below
- parents: int32 [8, 64], replicated, may hold values from -1 to 62, as said below
- path: int32 [8, 8], replicated, may hold values from 0 to 63, as said below
- accepted: int32 [8], replicated, may hold values from 1 to 8
Outputs:
- attn_out: bfloat16 [512, 8192], P('tp', 'seq')
- new_cache: bfloat16 [2, 8, 8192, 1024], P(None, None, 'seq', 'tp')
The draws below stay inside these ranges and needn't reach their ends.
Inputs may be any that keep to these rules, and one draw needn't show every extreme that they name: `lengths`: request r belongs to tenant t = r mod 4; a request of tenant t holds at most 8192 // 8 * 2 ** t - 8 tokens and at least half of that, and the first request of each tenant holds exactly that many. `parents`: node 0 is the root, with parent -1; every other node i has its parent among the nodes i - 7 to i - 1. `path`: for each request, the nodes of one branch of its tree, each the parent of the next, the last being node 63.
All inputs are finite; a program needn't handle non-finite values.
Results may differ from the reference program's by a relative error of at most 0.0051.
Values may be sent and summed in bfloat16 or wider, within the bound.
No kernel may reach another device: no remote copies, remote signals or barrier semaphores. Data moves between devices by JAX's collectives and lax.ppermute only.
A program may use at most 192 MiB of HBM per device.

```python
import jax
import jax.numpy as jnp
from jax import lax

D = 8192
HEADS = 64
KV_HEADS = 8
HEAD = 128
Q = 64
ACC = 8
CACHE_DEV = 1024
REQUESTS = 8
LMAX = 8192
ROWS = 512
SPAN = 7


def draw_queries(key, part):
    drawn = jnp.clip(jax.random.normal(jax.random.fold_in(key, 3), (ROWS, HEADS * HEAD), jnp.float32), -6.0, 6.0) * 2.5
    return drawn.astype(jnp.bfloat16)


def draw_cache(key, part):
    drawn = jnp.clip(jax.random.normal(jax.random.fold_in(key, 5), (2, REQUESTS, LMAX, KV_HEADS * HEAD), jnp.float32), -6.0, 6.0)
    return drawn.astype(jnp.bfloat16)


def draw_lengths(key, part):
    tenant = jnp.arange(REQUESTS, dtype=jnp.int32) % 4
    factors = jnp.array([1, 2, 4, 8], jnp.int32)
    ceiling = LMAX // 8 * factors[tenant] - ACC
    drawn = jax.random.randint(jax.random.fold_in(key, 9), (REQUESTS,), ceiling // 2, ceiling + 1)
    return jnp.where(jnp.arange(REQUESTS, dtype=jnp.int32) < 4, ceiling, drawn).astype(jnp.int32)


def tree_parents(key):
    node_ids = jnp.arange(Q, dtype=jnp.int32)
    reach_back = jnp.maximum(jnp.minimum(node_ids, SPAN), 1)
    step_back = jax.random.randint(jax.random.fold_in(key, 11), (REQUESTS, Q), 1, reach_back[None, :] + 1)
    return jnp.where(node_ids[None, :] == 0, -1, node_ids[None, :] - step_back).astype(jnp.int32)


def draw_parents(key, part):
    return tree_parents(key)


def draw_path(key, part):
    parent = tree_parents(key)

    def climb_up(current, unused):
        next_node = jnp.take_along_axis(parent, current[:, None], axis=1)[:, 0]
        return (next_node, current)
    deepest = jnp.full((REQUESTS,), Q - 1, jnp.int32)
    final_node, climbed = lax.scan(climb_up, deepest, None, length=ACC)
    return climbed[::-1].T.astype(jnp.int32)


def set_ends(values, stream_key, low, high):
    place = [jax.random.randint(jax.random.fold_in(stream_key, axis), (), 0, length) for axis, length in enumerate(values.shape)]
    longest = values.shape.index(max(values.shape))
    next_to = place[:longest] + [(place[longest] + 1) % values.shape[longest]] + place[longest + 1:]
    return values.at[tuple(place)].set(low).at[tuple(next_to)].set(high)


def level_of(key, shape, split, least, top_value):
    level, own = 1.0, jax.random.fold_in(key, 6)
    for axis_at, parts in split:
        steps = jnp.exp(jax.random.uniform(jax.random.fold_in(own, axis_at), (parts,), jnp.float32, least / len(split), top_value / len(split)))
        level = level * jnp.repeat(steps, shape[axis_at] // parts).reshape([-1 if axis == axis_at else 1 for axis in range(len(shape))])
    return level


def normal_values(stream_key, extent, deviation, most, cuts=(), kind=jnp.bfloat16):
    values = deviation * jax.random.normal(stream_key, extent, jnp.float32)
    if cuts:
        values = values * level_of(stream_key, extent, cuts, -0.22, 0.18)
    return jnp.clip(values, -most, most).astype(kind)


def setup_inputs(seed: int = 0) -> dict:
    keys = jax.random.split(jax.random.key(seed), 9)
    queries = draw_queries(jax.random.fold_in(keys[8], 71), 0)
    cache = draw_cache(jax.random.fold_in(keys[8], 71), 0)
    draft_kv = normal_values(keys[2], (2, ROWS, KV_HEADS * HEAD), 1.5, 9.0, ((1, 8), (2, 4)))
    out_weight = normal_values(keys[3], (D, D), D ** -0.5, 0.0625, ((0, 4), (1, 8)))
    lengths = draw_lengths(jax.random.fold_in(keys[8], 71), 0)
    parents = draw_parents(jax.random.fold_in(keys[8], 71), 0)
    path = draw_path(jax.random.fold_in(keys[8], 71), 0)
    accepted = set_ends(jax.random.randint(keys[7], (REQUESTS,), 1, ACC + 1), jax.random.fold_in(keys[7], 1), 1, ACC).astype(jnp.int32)
    return {"queries": queries, "cache": cache, "draft_kv": draft_kv, "out_weight": out_weight, "lengths": lengths, "parents": parents, "path": path, "accepted": accepted}


masked_score = -1.0e30


def ancestors(parents):
    node_count = parents.shape[1]
    node_ids = jnp.arange(node_count, dtype=jnp.int32)
    step_map = (parents[:, :, None] == node_ids[None, None, :]).astype(jnp.float32)
    identity = jnp.broadcast_to(jnp.eye(node_count, dtype=jnp.float32), step_map.shape)
    reached = jnp.minimum(identity + step_map, 1.0)
    for doubling in range((node_count - 1).bit_length()):
        squared = jnp.einsum("nij,njk->nik", reached, reached, precision=lax.Precision.HIGHEST)
        reached = jnp.minimum(squared, 1.0)
    return reached


def partial_block(query_rows, key_rows, value_rows, alive_mask):
    scores = jnp.einsum("qkge,pke->qkgp", query_rows.astype(jnp.float32), key_rows.astype(jnp.float32)) * (HEAD ** -0.5)
    masked = jnp.where(alive_mask, scores, masked_score)
    peak_score = jnp.max(masked, axis=-1)
    weights = jnp.where(alive_mask, jnp.exp(scores - peak_score[..., None]), 0.0)
    denominator = jnp.sum(weights, axis=-1)
    rounded = lax.optimization_barrier(weights.astype(jnp.bfloat16))
    weighted = jnp.einsum("qkgp,pke->qkge", rounded.astype(jnp.float32), value_rows.astype(jnp.float32))
    return peak_score, denominator, weighted


def join(former, latter):
    peak_score = jnp.maximum(former[0], latter[0])
    weight_former = jnp.exp(former[0] - peak_score)
    weight_latter = jnp.exp(latter[0] - peak_score)
    denominator = former[1] * weight_former + latter[1] * weight_latter
    weighted = former[2] * weight_former[..., None] + latter[2] * weight_latter[..., None]
    return peak_score, denominator, weighted


def reference(queries, cache, draft_kv, out_weight, lengths, parents, path, accepted):
    requests = lengths.shape[0]
    group_size = HEADS // KV_HEADS
    blocks = LMAX // CACHE_DEV
    reach = ancestors(parents)
    query_all = queries.reshape(requests, Q, KV_HEADS, group_size, HEAD)
    key_cache = cache[0].reshape(requests, blocks, CACHE_DEV, KV_HEADS, HEAD)
    value_cache = cache[1].reshape(requests, blocks, CACHE_DEV, KV_HEADS, HEAD)
    draft_table = draft_kv.reshape(2, requests, Q, KV_HEADS, HEAD)

    def one_request(inputs):
        query_rows, key_blocks, value_blocks, draft_keys, draft_values, reach_rows, length = inputs
        running = partial_block(query_rows, draft_keys, draft_values, reach_rows[:, None, None, :] > 0.5)

        def add_block(current, block_data):
            key_rows, value_rows, row_start = block_data
            alive_mask = (row_start + jnp.arange(CACHE_DEV, dtype=jnp.int32)) < length
            return join(current, partial_block(query_rows, key_rows, value_rows, alive_mask[None, None, None, :])), None

        starts = jnp.arange(blocks, dtype=jnp.int32) * CACHE_DEV
        running, unused = lax.scan(add_block, running, (key_blocks, value_blocks, starts))
        return (running[2] / running[1][..., None]).astype(jnp.bfloat16)

    attended = lax.map(one_request, (query_all, key_cache, value_cache, draft_table[0], draft_table[1], reach, lengths))
    attended = attended.reshape(requests * Q, HEADS * HEAD)
    attn_out = jnp.dot(attended, out_weight, preferred_element_type=jnp.float32).astype(jnp.bfloat16)

    draft_flat = draft_kv.reshape(2, requests, Q, KV_HEADS * HEAD)
    selector = (path[:, :, None] == jnp.arange(Q, dtype=jnp.int32)[None, None, :]).astype(jnp.float32)
    chosen = jnp.einsum("naq,xnqd->xnad", selector, draft_flat.astype(jnp.float32)).astype(jnp.bfloat16)
    slot_ids = lengths[:, None] + jnp.arange(ACC, dtype=jnp.int32)[None, :]
    owner_ids = jnp.broadcast_to(jnp.arange(requests, dtype=jnp.int32)[:, None], slot_ids.shape)
    previous = cache[:, owner_ids, slot_ids]
    keep_mask = (jnp.arange(ACC, dtype=jnp.int32)[None, :] < accepted[:, None])[None, :, :, None]
    new_cache = cache.at[:, owner_ids, slot_ids].set(jnp.where(keep_mask, chosen, previous))
    return attn_out, new_cache
```

```python
import functools
import math

import jax
import jax.numpy as jnp
from jax import lax
from jax.experimental import pallas as pl
from jax.experimental.pallas import tpu as pltpu
from jax.sharding import PartitionSpec as P

HEAD = 128
Q = 64
ACC = 8
TENANTS = 4
GROUP = 8
DEAD = -1e30
FOLD = HEAD**-0.5 * math.log2(math.e)
WINDOW = 32
BF = jnp.bfloat16
F32 = jnp.float32
VMEM = pl.BlockSpec(memory_space=pltpu.VMEM)
SMEM = pl.BlockSpec(memory_space=pltpu.SMEM)
ANY = pl.BlockSpec(memory_space=pl.ANY)
LIMIT = pltpu.CompilerParams(vmem_limit_bytes=48 * 1024 * 1024)


def dot(a, b, contract=((1,), (0,))):
    return lax.dot_general(a, b, (contract, ((), ())), preferred_element_type=F32)


def live_devices(tenant, n_seq):
    return max(1, n_seq * 2**tenant // 8)


def live_chips(tenant, n_seq):
    return max(1, live_devices(tenant, n_seq) // 2)


def pieces(x):
    high = x.astype(BF).astype(F32)
    middle = (x - high).astype(BF).astype(F32)
    return high, middle, (x - high - middle).astype(BF).astype(F32)


def stat_tile(columns):
    rows = columns[0].shape[0]
    lane = lax.broadcasted_iota(jnp.int32, (rows, HEAD), 1)
    tile = jnp.zeros((rows, HEAD), F32)
    for h, column in enumerate(columns):
        for k, piece in enumerate(pieces(column)):
            tile = jnp.where(lane == k * GROUP + h, piece, tile)
    return tile.astype(BF)


def attend_kernel(tenant, owners, sources, n_sources, *refs):
    len_ref, q_ref, kv_ref, parent_ref = refs[:4]
    drafts = refs[4 : 4 + n_sources]
    mine, theirs, m_s, l_s, acc_s, draft_s = refs[4 + n_sources :]
    span = kv_ref.shape[2]
    heads = q_ref.shape[1] // HEAD // 2
    half = heads * HEAD
    at = pl.program_id(0)
    r = tenant + TENANTS * at
    seq = lax.axis_index("seq")
    core = lax.rem(seq, 2)
    alive = len_ref[r] - seq * span
    owner = jnp.int32(owners[0])
    for k in range(1, len(owners)):
        owner = jnp.where(at == k, owners[k], owner)
    step = 2
    rows = step * Q

    def queries_of(g, h):
        return jnp.concatenate(
            [q_ref[:, (g * heads + h + j) * HEAD : (g * heads + h + j + 1) * HEAD] for j in range(step)], axis=0
        )

    def columns_of(g):
        kv = g * heads // GROUP
        return slice(kv * HEAD, (kv + 1) * HEAD)

    @pl.when(alive > 0)
    def _():
        lane = lax.broadcasted_iota(jnp.int32, (rows, span), 1)
        keep = lane < alive
        for g in range(2):
            keys = kv_ref[0, 0, :, columns_of(g)]
            values = kv_ref[1, 0, :, columns_of(g)]
            for h in range(0, heads, step):
                place = slice((g * heads + h) * Q, (g * heads + h + step) * Q)
                s = jnp.where(keep, dot(queries_of(g, h), keys, ((1,), (1,))), DEAD)
                m = jnp.max(s, axis=1, keepdims=True) * FOLD
                w = jnp.exp2(s * FOLD - m)
                l_s[place] = jnp.broadcast_to(jnp.sum(w, axis=1, keepdims=True), (rows, HEAD))
                m_s[place] = jnp.broadcast_to(m, (rows, HEAD))
                acc_s[place] = dot(w.astype(BF), values)

    @pl.when(alive <= 0)
    def _():
        m_s[...] = jnp.full_like(m_s, DEAD)
        l_s[...] = jnp.zeros_like(l_s)
        acc_s[...] = jnp.zeros_like(acc_s)

    @pl.when(seq == owner)
    def _():
        for k, source in enumerate(sources):

            @pl.when(at == k)
            def _():
                draft_s[...] = drafts[source][...]

        row_id = lax.broadcasted_iota(jnp.int32, (Q, Q), 0)
        column_id = lax.broadcasted_iota(jnp.int32, (Q, Q), 1)
        up = parent_ref[pl.ds(r, 1), :]
        reached = jnp.where((up == row_id) | (row_id == column_id), 1.0, 0.0).astype(BF)
        doublings = (Q - 1).bit_length()
        for k in range(doublings):
            contract = ((0,), (1,)) if k == doublings - 1 else ((1,), (0,))
            reached = jnp.minimum(dot(reached, reached, contract), 1.0).astype(BF)
        reach = jnp.concatenate([reached.astype(F32)] * step, axis=0) > 0.5
        for g in range(2):
            keys = draft_s[0, :, columns_of(g)]
            values = draft_s[1, :, columns_of(g)]
            for h in range(0, heads, step):
                place = slice((g * heads + h) * Q, (g * heads + h + step) * Q)
                s = jnp.where(reach, dot(queries_of(g, h), keys, ((1,), (1,))), DEAD)
                m_old = m_s[place]
                m = jnp.maximum(m_old, jnp.max(s, axis=1, keepdims=True) * FOLD)
                w = jnp.exp2(s * FOLD - m[:, :Q])
                shrink = jnp.exp2(m_old - m)
                l_s[place] = l_s[place] * shrink + jnp.sum(w, axis=1, keepdims=True)
                m_s[place] = m
                acc_s[place] = acc_s[place] * shrink + dot(w.astype(BF), values)

    def finish(g, out):
        stats = []
        for h in range(heads):
            place = slice((g * heads + h) * Q, (g * heads + h + 1) * Q)
            total = l_s[place]
            some = total > 0.0
            total = jnp.where(some, total, 1.0)
            out[:, h * HEAD : (h + 1) * HEAD] = (acc_s[place] / total).astype(BF)
            stats.append(jnp.where(some, m_s[place] + jnp.log2(total), DEAD))
        out[:, half:] = stat_tile(stats)

    for g in range(2):

        @pl.when(core == g)
        def _():
            finish(g, mine)
            finish(1 - g, theirs)


def attend(tenant, n_seq, queries, cache, parents, lengths, drafts, owners, sources):
    requests, span = cache.shape[1], cache.shape[2]
    count = requests // TENANTS
    used = sorted(set(sources))
    width, kv_width = queries.shape[1], cache.shape[3]
    wide = width // 2 + HEAD
    out = jax.ShapeDtypeStruct((count * Q, wide), BF)
    flops = 4 * count * Q * span * width
    return pl.pallas_call(
        functools.partial(attend_kernel, tenant, owners, [used.index(s) for s in sources], len(used)),
        grid_spec=pltpu.PrefetchScalarGridSpec(
            num_scalar_prefetch=1,
            grid=(count,),
            in_specs=[
                pl.BlockSpec((Q, width), lambda i, n: (tenant + TENANTS * i, 0)),
                pl.BlockSpec((2, 1, span, kv_width), lambda i, n: (0, tenant + TENANTS * i, 0, 0)),
                pl.BlockSpec((requests, Q), lambda i, n: (0, 0)),
            ]
            + [pl.BlockSpec((2, Q, kv_width), lambda i, n: (0, 0, 0)) for _ in used],
            out_specs=[pl.BlockSpec((Q, wide), lambda i, n: (i, 0))] * 2,
            scratch_shapes=[
                pltpu.VMEM((Q * width // HEAD, HEAD), F32),
                pltpu.VMEM((Q * width // HEAD, HEAD), F32),
                pltpu.VMEM((Q * width // HEAD, HEAD), F32),
                pltpu.VMEM((2, Q, kv_width), BF),
            ],
        ),
        out_shape=[out, out],
        compiler_params=LIMIT,
        cost_estimate=pl.CostEstimate(
            flops=flops, bytes_accessed=count * (4 * span * kv_width + 4 * Q * width), transcendentals=0
        ),
        name=f"attend_{tenant}",
    )(lengths, queries, cache, parents, *[drafts[s] for s in used])


def combine_kernel(final, a_ref, b_ref, out_ref):
    rows = a_ref.shape[0]
    half = a_ref.shape[1] - HEAD
    heads = half // HEAD

    def stats_of(ref):
        tile = ref[:, half:].astype(F32)
        return tile[:, :GROUP] + tile[:, GROUP : 2 * GROUP] + tile[:, 2 * GROUP : 3 * GROUP]

    a, b = stats_of(a_ref), stats_of(b_ref)
    top = jnp.maximum(a, b)
    weight_a, weight_b = jnp.exp2(a - top), jnp.exp2(b - top)
    total = weight_a + weight_b
    weight_a, weight_b = weight_a / total, weight_b / total
    level = top + jnp.log2(total)
    for h in range(heads):
        place = slice(h * HEAD, (h + 1) * HEAD)
        out_ref[:, place] = (
            a_ref[:, place].astype(F32) * weight_a[:, h : h + 1]
            + b_ref[:, place].astype(F32) * weight_b[:, h : h + 1]
        ).astype(BF)
    if not final:
        out_ref[:, half:] = stat_tile(
            [jnp.broadcast_to(level[:, h : h + 1], (rows, HEAD)) for h in range(heads)]
        )


def combine(a, b, final):
    rows, wide = a.shape
    return pl.pallas_call(
        functools.partial(combine_kernel, final),
        out_shape=jax.ShapeDtypeStruct((rows, wide - HEAD if final else wide), BF),
        in_specs=[VMEM, VMEM],
        out_specs=VMEM,
        compiler_params=LIMIT,
        cost_estimate=pl.CostEstimate(flops=rows * wide * 8, bytes_accessed=rows * wide * 6, transcendentals=0),
        name="combine",
    )(a, b)


def project_kernel(requests, n_tp, tenants, *refs):
    count = len(tenants)
    parts = refs[: 2 * count]
    w_ref = refs[2 * count]
    own_ref, outs, product = refs[2 * count + 1], refs[2 * count + 2 : -1], refs[-1]
    tp = lax.axis_index("tp")
    core = lax.rem(lax.axis_index("seq"), 2)
    half = w_ref.shape[0] // 2
    near = w_ref[pl.ds(pl.multiple_of(core * half, half), half), :]
    far = w_ref[pl.ds(pl.multiple_of((1 - core) * half, half), half), :]
    mine = jnp.concatenate([parts[2 * k][...] for k in range(count)], axis=0)
    other = jnp.concatenate([parts[2 * k + 1][...] for k in range(count)], axis=0)
    product[...] = dot(mine, near) + dot(other, far)
    each = requests // TENANTS
    share = requests // n_tp
    taken = {}
    for k, tenant in enumerate(tenants):
        for i in range(each):
            r = tenant + TENANTS * i
            taken.setdefault(r // share, []).append((r % share, k * each + i))
    for owner in range(n_tp):
        for slot in range(n_tp):

            @pl.when((owner ^ tp) == slot)
            def _():
                for place, (_, block) in enumerate(sorted(taken[owner])):
                    value = product[block * Q : (block + 1) * Q, :]
                    target = own_ref if slot == 0 else outs[slot - 1]
                    target[place * Q : (place + 1) * Q, :] = value.astype(target.dtype)


def project(requests, n_tp, tenants, parts, weight):
    depth, columns = weight.shape
    rows = len(tenants) * (requests // TENANTS) * Q
    mine = rows // n_tp
    steps = 4 if columns % (4 * HEAD) == 0 else 1
    wide = columns // steps
    return pl.pallas_call(
        functools.partial(project_kernel, requests, n_tp, tenants),
        grid=(steps,),
        in_specs=[pl.BlockSpec(part.shape, lambda i: (0, 0)) for part in parts]
        + [pl.BlockSpec((depth, wide), lambda i: (0, i))],
        out_specs=[pl.BlockSpec((mine, wide), lambda i: (0, i))] * n_tp,
        out_shape=[jax.ShapeDtypeStruct((mine, columns), F32)]
        + [jax.ShapeDtypeStruct((mine, columns), BF)] * (n_tp - 1),
        scratch_shapes=[pltpu.VMEM((rows, wide), F32)],
        compiler_params=LIMIT,
        cost_estimate=pl.CostEstimate(
            flops=2 * rows * depth * columns, bytes_accessed=2 * depth * columns, transcendentals=0
        ),
        name="project",
    )(*parts, weight)


def choose_kernel(path_ref, draft_ref, out_ref):
    seq = lax.axis_index("seq")
    row = lax.broadcasted_iota(jnp.int32, (ACC, Q), 0)
    column = lax.broadcasted_iota(jnp.int32, (ACC, Q), 1)
    picked = jnp.zeros((ACC, Q), jnp.int32)
    for j in range(ACC):
        picked = jnp.where(row == j, path_ref[seq, j], picked)
    selector = jnp.where(picked == column, 1.0, 0.0).astype(BF)
    for x in range(2):
        out_ref[0, x] = dot(selector, draft_ref[x]).astype(BF)


def choose(path, draft_kv):
    return pl.pallas_call(
        choose_kernel,
        out_shape=jax.ShapeDtypeStruct((1, 2, ACC, draft_kv.shape[2]), BF),
        in_specs=[SMEM, VMEM],
        out_specs=VMEM,
        compiler_params=LIMIT,
        name="choose",
    )(path, draft_kv)


def copy_kernel(cache_ref, out_ref):
    out_ref[...] = cache_ref[...]


def copied(cache):
    _, requests, span, width = cache.shape
    block = pl.BlockSpec((2, 1, span, width), lambda i: (0, i, 0, 0))
    return pl.pallas_call(
        copy_kernel,
        grid=(requests,),
        out_shape=jax.ShapeDtypeStruct(cache.shape, BF),
        in_specs=[block],
        out_specs=block,
        compiler_params=LIMIT,
        cost_estimate=pl.CostEstimate(flops=0, bytes_accessed=4 * math.prod(cache.shape), transcendentals=0),
        name="copy_cache",
    )(cache)


def patch_kernel(len_ref, accept_ref, cache_ref, chosen_ref, out_ref, window, load_sem, store_sem):
    requests, span = cache_ref.shape[1], cache_ref.shape[2]
    seq = lax.axis_index("seq")

    def place_of(r):
        first = len_ref[r] - seq * span
        start = jnp.clip(first // 16 * 16, 0, span - WINDOW)
        return first, pl.multiple_of(start, 16), (first + ACC > 0) & (first < span)

    def load(r):
        _, start, here = place_of(r)
        return here, pltpu.make_async_copy(
            cache_ref.at[:, r, pl.ds(start, WINDOW), :], window.at[r], load_sem.at[r]
        )

    def store(r):
        _, start, here = place_of(r)
        return here, pltpu.make_async_copy(
            window.at[r], out_ref.at[:, r, pl.ds(start, WINDOW), :], store_sem.at[r]
        )

    for r in range(requests):
        here, copy = load(r)
        pl.when(here)(copy.start)
    for r in range(requests):
        here, copy = load(r)
        first, start, _ = place_of(r)

        @pl.when(here)
        def _():
            copy.wait()
            row = lax.broadcasted_iota(jnp.int32, window.shape[2:], 0) + (start - first)
            for x in range(2):
                value = window[r, x].astype(F32)
                rows = chosen_ref[r ^ seq, x].astype(F32)
                for j in range(ACC):
                    value = jnp.where((row == j) & (j < accept_ref[r]), rows[j : j + 1], value)
                window[r, x] = value.astype(BF)
            store(r)[1].start()

    for r in range(requests):
        here, copy = store(r)
        pl.when(here)(copy.wait)


def patched(cache, chosen, lengths, accepted):
    requests = cache.shape[1]
    return pl.pallas_call(
        patch_kernel,
        out_shape=jax.ShapeDtypeStruct(cache.shape, BF),
        in_specs=[SMEM, SMEM, ANY, VMEM],
        out_specs=ANY,
        scratch_shapes=[
            pltpu.VMEM((requests, 2, WINDOW, cache.shape[3]), BF),
            pltpu.SemaphoreType.DMA((requests,)),
            pltpu.SemaphoreType.DMA((requests,)),
        ],
        input_output_aliases={2: 0},
        compiler_params=LIMIT,
        name="patch_cache",
    )(lengths, accepted, cache, chosen)


def chip_pairs(pairs):
    return [(2 * a + c, 2 * b + c) for a, b in pairs for c in range(2)]


def local(n_seq, n_tp, queries, cache, draft_kv, out_weight, lengths, parents, path, accepted):
    requests = cache.shape[1]
    chips = n_seq // 2
    seq = lax.axis_index("seq")
    chip = seq // 2
    swap_pairs = [(s, s ^ 1) for s in range(n_seq)]

    def swap(array):
        return lax.ppermute(array, "seq", swap_pairs)

    def send(array, pairs):
        return lax.ppermute(array, "seq", chip_pairs(pairs))

    owners, sources, rounds = {}, {}, []
    for r in range(requests):
        owners[r] = r % live_devices(r % TENANTS, n_seq)
        sources[r] = 0
        if owners[r] != r:
            for k, taken in enumerate(rounds):
                if all(owners[r] != b for _, b in taken):
                    break
            else:
                k = len(rounds)
                rounds.append([])
            rounds[k].append((r, owners[r]))
            sources[r] = k + 1
    drafts = [draft_kv] + [lax.ppermute(draft_kv, "seq", pairs) for pairs in rounds]

    def partial_of(tenant):
        own = range(tenant, requests, TENANTS)
        return attend(
            tenant, n_seq, queries, cache, parents, lengths, drafts, [owners[r] for r in own], [sources[r] for r in own]
        )

    def spread(value, first, last):
        held = [value]
        inside = (chip >= first) & (chip <= last)
        newest = value
        while first > 0 or last < chips - 1:
            pairs = []
            if first > 0:
                pairs.append((first, first - 1))
                first -= 1
            if last < chips - 1:
                pairs.append((last, last + 1))
                last += 1
            newest = send(newest, pairs)
            held.append(newest)
        if len(held) == 1:
            return value
        rest = functools.reduce(jnp.add, held[1:])
        return jnp.where(inside, value, rest)

    def reduced(tenant):
        mine, theirs = partial_of(tenant)
        count = live_chips(tenant, n_seq)
        value = combine(mine, swap(theirs), count == 1)
        if count == 1:
            return value, 0, 0
        half = count // 2
        for k in range(half - 1):
            value = combine(value, send(value, [(k, k + 1), (count - 1 - k, count - 2 - k)]), False)
        value = combine(value, send(value, [(half - 1, half), (half, half - 1)]), True)
        return value, half - 1, half

    whole = {}
    for tenant in (3, 2, 0, 1):
        value = spread(*reduced(tenant))
        whole[tenant] = (value, swap(value))

    def sums(tenants):
        parts = [part for tenant in tenants for part in whole[tenant]]
        own, *others = project(requests, n_tp, tenants, parts, out_weight)
        for k, other in enumerate(others):
            arrived = lax.ppermute(other, "tp", [(t, t ^ (k + 1)) for t in range(n_tp)])
            own = own + arrived.astype(F32)
        return own.astype(BF)

    columns = out_weight.shape[1]
    even, odd = (sums(tenants).reshape(-1, Q, columns) for tenants in ((0, 2), (1, 3)))
    attn_out = jnp.stack([even, odd], axis=1).reshape(-1, columns)

    chosen = choose(path, draft_kv)
    distance = 1
    while distance < n_seq:
        arrived = lax.ppermute(chosen, "seq", [(s, s ^ distance) for s in range(n_seq)])
        chosen = jnp.concatenate([chosen, arrived], axis=0)
        distance *= 2
    new_cache = patched(copied(cache), chosen, lengths, accepted)
    return attn_out, new_cache


def solution(mesh):
    return jax.shard_map(
        functools.partial(local, mesh.shape["seq"], mesh.shape["tp"]),
        mesh=mesh,
        in_specs=(
            P(None, "tp"),
            P(None, None, "seq", "tp"),
            P(None, "seq", "tp"),
            P("tp", "seq"),
            P(),
            P(),
            P(),
            P(),
        ),
        out_specs=(P("tp", "seq"), P(None, None, "seq", "tp")),
        check_vma=False,
    )
```

```python
import functools
import math

import jax
import jax.numpy as jnp
from jax import lax
from jax.experimental import pallas as pl
from jax.experimental.pallas import tpu as pltpu
from jax.sharding import PartitionSpec as P

HEAD = 128
Q = 64
ACC = 8
TENANTS = 4
GROUP = 8
DEAD = -1e30
FOLD = HEAD**-0.5 * math.log2(math.e)
WINDOW = 32
BF = jnp.bfloat16
F32 = jnp.float32
VMEM = pl.BlockSpec(memory_space=pltpu.VMEM)
SMEM = pl.BlockSpec(memory_space=pltpu.SMEM)
ANY = pl.BlockSpec(memory_space=pl.ANY)
HBM = pl.BlockSpec(memory_space=pltpu.HBM)
SMALL = pl.CostEstimate(flops=1, bytes_accessed=1, transcendentals=0)


def limit(mebibytes):
    return pltpu.CompilerParams(vmem_limit_bytes=mebibytes * 1024 * 1024)


def dot(a, b, contract=((1,), (0,))):
    return lax.dot_general(a, b, (contract, ((), ())), preferred_element_type=F32)


def live_devices(tenant, n_seq):
    return max(1, n_seq * 2**tenant // 8)


def live_chips(tenant, n_seq):
    return max(1, live_devices(tenant, n_seq) // 2)


def pieces(x):
    high = x.astype(BF).astype(F32)
    middle = (x - high).astype(BF).astype(F32)
    return high, middle, (x - high - middle).astype(BF).astype(F32)


def stat_tile(columns):
    rows = columns[0].shape[0]
    lane = lax.broadcasted_iota(jnp.int32, (rows, HEAD), 1)
    tile = jnp.zeros((rows, HEAD), F32)
    for h, column in enumerate(columns):
        for k, piece in enumerate(pieces(column)):
            tile = jnp.where(lane == k * GROUP + h, piece, tile)
    return tile.astype(BF)


def reach_kernel(parent_ref, out_ref):
    requests = parent_ref.shape[0]
    row_id = lax.broadcasted_iota(jnp.int32, (2 * Q, 2 * Q), 0)
    column_id = lax.broadcasted_iota(jnp.int32, (2 * Q, 2 * Q), 1)
    chains = []
    for r in range(0, requests, 2):
        up = []
        for k in range(2):
            parent = parent_ref[r + k : r + k + 1, :]
            up.append(jnp.where(parent < 0, -1, parent + k * Q))
        linked = (jnp.concatenate(up, axis=1) == row_id) | (row_id == column_id)
        chains.append(jnp.where(linked, 1.0, 0.0).astype(BF))
    doublings = (Q - 1).bit_length()
    for k in range(doublings):
        contract = ((0,), (1,)) if k == doublings - 1 else ((1,), (0,))
        chains = [jnp.minimum(dot(chain, chain, contract), 1.0).astype(BF) for chain in chains]
    for r in range(requests):
        k = r % 2 * Q
        out_ref[r] = chains[r // 2].astype(F32)[k : k + Q, k : k + Q]


def reach_of(parents):
    return pl.pallas_call(
        reach_kernel,
        out_shape=jax.ShapeDtypeStruct((parents.shape[0], Q, Q), F32),
        in_specs=[VMEM],
        out_specs=VMEM,
        compiler_params=limit(8),
        cost_estimate=SMALL,
        name="reach",
    )(parents)


def attend_kernel(tenant, owners, sources, n_sources, n_after, resident, *refs):
    len_ref, q_ref, kv_ref, reach_ref = refs[:4]
    drafts = refs[4 : 4 + n_sources]
    outs = refs[4 + n_sources + n_after :]
    mine, theirs, copy_ref, len_s, q_s, kv_s, draft_s, m_s, l_s, acc_s, load, store = outs
    count = draft_s.shape[0]
    span = kv_ref.shape[2]
    heads = q_ref.shape[1] // HEAD // 2
    half = heads * HEAD
    rows = heads * Q
    seq = lax.axis_index("seq")
    core = lax.rem(seq, 2)

    def loads(i):
        r = tenant + TENANTS * i
        if resident:
            return []
        return [
            pltpu.make_async_copy(q_ref.at[pl.ds(r * Q, Q), :], q_s.at[i], load.at[i, 0]),
            pltpu.make_async_copy(kv_ref.at[0, r], kv_s.at[i, 0], load.at[i, 1]),
            pltpu.make_async_copy(kv_ref.at[1, r], kv_s.at[i, 1], load.at[i, 2]),
        ]

    def stored(i):
        r = tenant + TENANTS * i
        return pltpu.make_async_copy(kv_ref.at[:, r] if resident else kv_s.at[i], copy_ref.at[:, r], store.at[i])

    def cached(i, x, columns):
        return kv_ref[x, tenant + TENANTS * i, :, columns] if resident else kv_s[i, x, :, columns]

    small = [pltpu.make_async_copy(len_ref, len_s, load.at[count, 0])]
    given = [pltpu.make_async_copy(drafts[sources[i]], draft_s.at[i], load.at[i, 3]) for i in range(count)]
    for copy in (*loads(0), *small, *[c for i in range(1, count) for c in loads(i)], *given):
        copy.start()
    for copy in small:
        copy.wait()

    def columns_of(g):
        kv = g * heads // GROUP
        return slice(kv * HEAD, (kv + 1) * HEAD)

    for i in range(count):
        r = tenant + TENANTS * i
        alive = len_s[r] - seq * span
        for copy in loads(i):
            copy.wait()
        given[i].wait()
        stored(i).start()

        def queries_of(g):
            held = q_ref.at[pl.ds(r * Q, Q)] if resident else q_s.at[i]
            return jnp.concatenate(
                [held[:, (g * heads + h) * HEAD : (g * heads + h + 1) * HEAD] for h in range(heads)], axis=0
            )

        @pl.when(alive > 0)
        def _():
            keep = lax.broadcasted_iota(jnp.int32, (span, HEAD), 0) < alive
            ones = jnp.where(keep, 1.0, 0.0).astype(BF)

            def scores(g):
                keys = cached(i, 0, columns_of(g))
                keys = jnp.where(keep, keys, jnp.broadcast_to(keys[:1], keys.shape))
                return dot(queries_of(g), keys, ((1,), (1,)))

            def weigh(g, m, w):
                values = cached(i, 1, columns_of(g))
                values = jnp.where(keep, values, jnp.zeros_like(values))
                o = dot(w, jnp.concatenate([values, ones], axis=1))
                place = slice(g * rows, (g + 1) * rows)
                m_s[place] = jnp.broadcast_to(m, (rows, HEAD))
                acc_s[place] = o[:, :HEAD]
                l_s[place] = o[:, HEAD:]

            upcoming = scores(0)
            pending = None
            for g in range(2):
                s = upcoming
                if g == 0:
                    upcoming = scores(1)
                m = jnp.max(s, axis=1, keepdims=True) * FOLD
                w = jnp.exp2(s * FOLD - m).astype(BF)
                if pending is not None:
                    weigh(*pending)
                pending = (g, m, w)
            weigh(*pending)

        @pl.when(alive <= 0)
        def _():
            m_s[...] = jnp.full_like(m_s, DEAD)
            l_s[...] = jnp.zeros_like(l_s)
            acc_s[...] = jnp.zeros_like(acc_s)

        @pl.when(seq == owners[i])
        def _():
            reach = jnp.concatenate([reach_ref[r]] * heads, axis=0) > 0.5
            for g in range(2):
                place = slice(g * rows, (g + 1) * rows)
                s = dot(queries_of(g), draft_s[i, 0, :, columns_of(g)], ((1,), (1,)))
                s = jnp.where(reach, s, DEAD)
                m_old = m_s[place]
                m = jnp.maximum(m_old, jnp.max(s, axis=1, keepdims=True) * FOLD)
                w = jnp.exp2(s * FOLD - m[:, :Q])
                shrink = jnp.exp2(m_old - m)
                l_s[place] = l_s[place] * shrink + jnp.sum(w, axis=1, keepdims=True)
                m_s[place] = m
                acc_s[place] = acc_s[place] * shrink + dot(w.astype(BF), draft_s[i, 1, :, columns_of(g)])

        def finish(g, out):
            stats = []
            for h in range(heads):
                place = slice((g * heads + h) * Q, (g * heads + h + 1) * Q)
                total = l_s[place]
                some = total > 0.0
                total = jnp.where(some, total, 1.0)
                out[i * Q : (i + 1) * Q, h * HEAD : (h + 1) * HEAD] = (acc_s[place] / total).astype(BF)
                stats.append(jnp.where(some, m_s[place] + jnp.log2(total), DEAD))
            out[i * Q : (i + 1) * Q, half:] = stat_tile(stats)

        for g in range(2):

            @pl.when(core == g)
            def _():
                finish(g, mine)
                finish(1 - g, theirs)

    for i in range(count):
        stored(i).wait()


def attend(tenant, queries, cache, reach, lengths, drafts, owners, sources, copy, after, resident=False):
    requests, span = cache.shape[1], cache.shape[2]
    count = requests // TENANTS
    used = sorted(set(sources))
    width, kv_width = queries.shape[1], cache.shape[3]
    wide = width // 2 + HEAD
    out = jax.ShapeDtypeStruct((count * Q, wide), BF)
    carried = [] if copy is None else [copy]
    extra = list(after) + carried
    return pl.pallas_call(
        functools.partial(attend_kernel, tenant, owners, [used.index(s) for s in sources], len(used), len(extra), resident),
        in_specs=[HBM] + [VMEM if resident else HBM] * 2 + [VMEM] + [HBM] * len(used) + [ANY] * len(extra),
        out_specs=[VMEM, VMEM, ANY],
        scratch_shapes=[
            pltpu.SMEM((requests,), jnp.int32),
            pltpu.VMEM((1 if resident else count, Q, width), BF),
            pltpu.VMEM((1, 1, 16, HEAD) if resident else (count, 2, span, kv_width), BF),
            pltpu.VMEM((count, 2, Q, kv_width), BF),
            pltpu.VMEM((Q * width // HEAD, HEAD), F32),
            pltpu.VMEM((Q * width // HEAD, HEAD), F32),
            pltpu.VMEM((Q * width // HEAD, HEAD), F32),
            pltpu.SemaphoreType.DMA((count + 1, 4)),
            pltpu.SemaphoreType.DMA((count,)),
        ],
        out_shape=[out, out, jax.ShapeDtypeStruct(cache.shape, BF)],
        input_output_aliases={3 + len(used) + len(extra): 2} if carried else {},
        compiler_params=limit(28),
        cost_estimate=SMALL,
        name=f"attend_{tenant}",
    )(lengths, queries, cache, reach, *[drafts[s] for s in used], *extra)


def combine_kernel(final, a_ref, b_ref, *rest):
    out_ref = rest[-1]
    rows = a_ref.shape[0]
    half = a_ref.shape[1] - HEAD
    heads = half // HEAD

    def stats_of(ref):
        tile = ref[:, half:].astype(F32)
        return tile[:, :GROUP] + tile[:, GROUP : 2 * GROUP] + tile[:, 2 * GROUP : 3 * GROUP]

    a, b = stats_of(a_ref), stats_of(b_ref)
    top = jnp.maximum(a, b)
    weight_a, weight_b = jnp.exp2(a - top), jnp.exp2(b - top)
    total = weight_a + weight_b
    weight_a, weight_b = weight_a / total, weight_b / total
    level = top + jnp.log2(total)
    for h in range(heads):
        place = slice(h * HEAD, (h + 1) * HEAD)
        out_ref[:, place] = (
            a_ref[:, place].astype(F32) * weight_a[:, h : h + 1]
            + b_ref[:, place].astype(F32) * weight_b[:, h : h + 1]
        ).astype(BF)
    if not final:
        out_ref[:, half:] = stat_tile(
            [jnp.broadcast_to(level[:, h : h + 1], (rows, HEAD)) for h in range(heads)]
        )


def combine(a, b, final, after=()):
    rows, wide = a.shape
    return pl.pallas_call(
        functools.partial(combine_kernel, final),
        out_shape=jax.ShapeDtypeStruct((rows, wide - HEAD if final else wide), BF),
        in_specs=[VMEM, VMEM] + [ANY for _ in after],
        out_specs=VMEM,
        compiler_params=limit(8),
        cost_estimate=SMALL,
        name="combine",
    )(a, b, *after)


def project_kernel(requests, n_tp, tenants, n_after, *refs):
    count = len(tenants)
    parts = refs[: 2 * count]
    w_ref = refs[2 * count]
    own_ref, *outs = refs[2 * count + 1 + n_after : -1]
    product = refs[-1]
    tp = lax.axis_index("tp")
    core = lax.rem(lax.axis_index("seq"), 2)
    half = w_ref.shape[0] // 2
    mine = jnp.concatenate([parts[2 * k][...] for k in range(count)], axis=0)
    other = jnp.concatenate([parts[2 * k + 1][...] for k in range(count)], axis=0)
    near = pl.ds(pl.multiple_of(core * half, half), half)
    far = pl.ds(pl.multiple_of((1 - core) * half, half), half)
    product[...] = dot(mine, w_ref[near, :]) + dot(other, w_ref[far, :])
    each = requests // TENANTS
    share = requests // n_tp
    taken = {}
    for k, tenant in enumerate(tenants):
        for i in range(each):
            r = tenant + TENANTS * i
            taken.setdefault(r // share, []).append((r % share, k * each + i))
    for owner in range(n_tp):
        for slot in range(n_tp):

            @pl.when((owner ^ tp) == slot)
            def _():
                for place, (_, block) in enumerate(sorted(taken[owner])):
                    value = product[block * Q : (block + 1) * Q, :]
                    target = own_ref if slot == 0 else outs[slot - 1]
                    target[place * Q : (place + 1) * Q, :] = value.astype(target.dtype)


def project(requests, n_tp, tenants, parts, weight, after):
    depth, columns = weight.shape
    rows = len(tenants) * (requests // TENANTS) * Q
    mine = rows // n_tp
    return pl.pallas_call(
        functools.partial(project_kernel, requests, n_tp, tenants, len(after)),
        in_specs=[VMEM] * (len(parts) + 1) + [ANY] * len(after),
        out_specs=[VMEM] * n_tp,
        out_shape=[jax.ShapeDtypeStruct((mine, columns), F32)]
        + [jax.ShapeDtypeStruct((mine, columns), BF)] * (n_tp - 1),
        scratch_shapes=[pltpu.VMEM((rows, columns), F32)],
        compiler_params=limit(20),
        cost_estimate=SMALL,
        name="project",
    )(*parts, weight, *after)


def pick_kernel(n_tokens, first, last, *refs):
    out_ref = refs[-1]
    value, *others = refs[: len(refs) - 1 - n_tokens]
    chip = lax.axis_index("seq") // 2
    inside = (chip >= first) & (chip <= last)

    @pl.when(inside)
    def _():
        out_ref[...] = value[...]

    @pl.when(jnp.logical_not(inside))
    def _():
        out_ref[...] = functools.reduce(jnp.add, [other[...] for other in others])


def pick(value, others, first, last, after):
    return pl.pallas_call(
        functools.partial(pick_kernel, len(after), first, last),
        out_shape=jax.ShapeDtypeStruct(value.shape, BF),
        in_specs=[VMEM] * (1 + len(others)) + [ANY] * len(after),
        out_specs=VMEM,
        compiler_params=limit(8),
        cost_estimate=SMALL,
        name="pick",
    )(value, *others, *after)


def stack_kernel(a_ref, b_ref, *rest):
    out_ref = rest[-1]
    size = a_ref.shape[0]
    out_ref[:size] = a_ref[...]
    out_ref[size:] = b_ref[...]


def stack(a, b, after):
    return pl.pallas_call(
        stack_kernel,
        out_shape=jax.ShapeDtypeStruct((2 * a.shape[0], *a.shape[1:]), BF),
        in_specs=[VMEM, VMEM] + [ANY] * len(after),
        out_specs=VMEM,
        compiler_params=limit(4),
        cost_estimate=SMALL,
        name="stack",
    )(a, b, *after)


def choose_kernel(path_ref, draft_ref, out_ref):
    seq = lax.axis_index("seq")
    row = lax.broadcasted_iota(jnp.int32, (ACC, Q), 0)
    column = lax.broadcasted_iota(jnp.int32, (ACC, Q), 1)
    picked = jnp.zeros((ACC, Q), jnp.int32)
    for j in range(ACC):
        picked = jnp.where(row == j, path_ref[seq, j], picked)
    selector = jnp.where(picked == column, 1.0, 0.0).astype(BF)
    for x in range(2):
        out_ref[0, x] = dot(selector, draft_ref[x]).astype(BF)


def choose(path, draft_kv):
    return pl.pallas_call(
        choose_kernel,
        out_shape=jax.ShapeDtypeStruct((1, 2, ACC, draft_kv.shape[2]), BF),
        in_specs=[SMEM, VMEM],
        out_specs=VMEM,
        compiler_params=limit(4),
        name="choose",
    )(path, draft_kv)


def patch_kernel(len_ref, accept_ref, cache_ref, chosen_ref, out_ref, window, load_sem, store_sem):
    requests, span = cache_ref.shape[1], cache_ref.shape[2]
    seq = lax.axis_index("seq")

    def place_of(r):
        first = len_ref[r] - seq * span
        start = jnp.clip(first // 16 * 16, 0, span - WINDOW)
        return first, pl.multiple_of(start, 16), (first + ACC > 0) & (first < span)

    def load(r):
        _, start, here = place_of(r)
        return here, pltpu.make_async_copy(
            cache_ref.at[:, r, pl.ds(start, WINDOW), :], window.at[r], load_sem.at[r]
        )

    def store(r):
        _, start, here = place_of(r)
        return here, pltpu.make_async_copy(
            window.at[r], out_ref.at[:, r, pl.ds(start, WINDOW), :], store_sem.at[r]
        )

    for r in range(requests):
        here, copy = load(r)
        pl.when(here)(copy.start)
    for r in range(requests):
        here, copy = load(r)
        first, start, _ = place_of(r)

        @pl.when(here)
        def _():
            copy.wait()
            row = lax.broadcasted_iota(jnp.int32, window.shape[2:], 0) + (start - first)
            for x in range(2):
                value = window[r, x].astype(F32)
                rows = chosen_ref[r ^ seq, x].astype(F32)
                for j in range(ACC):
                    value = jnp.where((row == j) & (j < accept_ref[r]), rows[j : j + 1], value)
                window[r, x] = value.astype(BF)
            store(r)[1].start()

    for r in range(requests):
        here, copy = store(r)
        pl.when(here)(copy.wait)


def patched(cache, chosen, lengths, accepted):
    requests = cache.shape[1]
    return pl.pallas_call(
        patch_kernel,
        out_shape=jax.ShapeDtypeStruct(cache.shape, BF),
        in_specs=[SMEM, SMEM, ANY, VMEM],
        out_specs=ANY,
        scratch_shapes=[
            pltpu.VMEM((requests, 2, WINDOW, cache.shape[3]), BF),
            pltpu.SemaphoreType.DMA((requests,)),
            pltpu.SemaphoreType.DMA((requests,)),
        ],
        input_output_aliases={2: 0},
        compiler_params=limit(8),
        name="patch_cache",
    )(lengths, accepted, cache, chosen)


def chip_pairs(pairs):
    return [(2 * a + c, 2 * b + c) for a, b in pairs for c in range(2)]


def local(n_seq, n_tp, queries, cache, draft_kv, out_weight, lengths, parents, path, accepted):
    requests = cache.shape[1]
    chips = n_seq // 2
    seq = lax.axis_index("seq")
    chip = seq // 2
    swap_pairs = [(s, s ^ 1) for s in range(n_seq)]

    def swap(array):
        return lax.ppermute(array, "seq", swap_pairs)

    def send(array, pairs):
        return lax.ppermute(array, "seq", chip_pairs(pairs))

    owners, sources, rounds = {}, {}, []
    for r in range(requests):
        owners[r] = r % live_devices(r % TENANTS, n_seq)
        sources[r] = 0
        if owners[r] != r:
            for k, taken in enumerate(rounds):
                if all(owners[r] != b for _, b in taken):
                    break
            else:
                k = len(rounds)
                rounds.append([])
            rounds[k].append((r, owners[r]))
            sources[r] = k + 1
    drafts = [draft_kv] + [lax.ppermute(draft_kv, "seq", pairs) for pairs in rounds]

    copy = None

    reach = reach_of(parents)

    def partial_of(tenant, after=()):
        nonlocal copy
        own = range(tenant, requests, TENANTS)
        mine, theirs, copy = attend(
            tenant,
            queries,
            cache,
            reach,
            lengths,
            drafts,
            [owners[r] for r in own],
            [sources[r] for r in own],
            copy,
            list(after),
            resident=tenant != 3,
        )
        return mine, swap(theirs)

    count = {tenant: live_chips(tenant, n_seq) for tenant in range(TENANTS)}
    steps, value = {}, {}
    for tenant in range(TENANTS):
        last, half = count[tenant] - 1, count[tenant] // 2
        steps[tenant] = [[(k, k + 1), (last - k, last - k - 1)] for k in range(half)]

    def join(tenant, pair, after=()):
        value[tenant] = combine(*pair, count[tenant] == 1, after)

    def advance(tenant, after=()):
        if steps[tenant]:
            arrived = send(value[tenant], steps[tenant].pop(0))
            value[tenant] = combine(value[tenant], arrived, not steps[tenant], after)

    def spread(tenant, after=()):
        first = max(count[tenant] // 2 - 1, 0)
        last = count[tenant] // 2
        inside = (chip >= first) & (chip <= last)
        top = (first, last)
        newest = value[tenant]
        if chips == 4 and last == 0:
            newest = send(newest, [(0, 2)])
            held = [newest, send(newest, [(2, 1)]), send(newest, [(2, 3)])]
        else:
            held = []
            while first > 0 or last < chips - 1:
                pairs = []
                if first > 0:
                    pairs.append((first, first - 1))
                    first -= 1
                if last < chips - 1:
                    pairs.append((last, last + 1))
                    last += 1
                newest = send(newest, pairs)
                held.append(newest)
        if held and after:
            value[tenant] = pick(value[tenant], held, top[0], top[1], after)
        elif held:
            value[tenant] = jnp.where(inside, value[tenant], functools.reduce(jnp.add, held))

    join(3, partial_of(3))
    zero = partial_of(0, [value[3]])
    advance(3, [zero[0]])
    join(0, zero, [value[3]])
    two = partial_of(2, [value[0]])
    join(2, two)
    one = partial_of(1, [value[2]])
    advance(3, [one[0]])
    advance(2, [value[3]])
    join(1, one, [value[2]])
    whole = {}
    for tenant in (3, 0, 2, 1):
        while steps[tenant]:
            advance(tenant, [value[1]])

    def sums(tenants, after):
        parts = [part for tenant in tenants for part in whole[tenant]]
        own, *others = project(requests, n_tp, tenants, parts, out_weight, after)
        arrived = [
            lax.ppermute(other, "tp", [(t, t ^ (k + 1)) for t in range(n_tp)]).astype(F32)
            for k, other in enumerate(others)
        ]
        return own, functools.reduce(jnp.add, arrived, own).astype(BF)

    for tenant in (3, 0):
        spread(tenant)
        whole[tenant] = (value[tenant], swap(value[tenant]))
    own, one_sum = sums((3, 0), [])
    for tenant in (2, 1):
        spread(tenant, [own])
        whole[tenant] = (value[tenant], swap(value[tenant]))
    _, other_sum = sums((2, 1), [one_sum])

    assert requests == 2 * n_tp
    even = lax.axis_index("tp") % 2 == 0
    attn_out = jnp.concatenate(
        [jnp.where(even, one_sum, other_sum), jnp.where(even, other_sum, one_sum)], axis=0
    )

    chosen = choose(path, draft_kv)
    distance = 1
    while distance < n_seq:
        arrived = lax.ppermute(chosen, "seq", [(s, s ^ distance) for s in range(n_seq)])
        chosen = jnp.concatenate([chosen, arrived], axis=0)
        distance *= 2
    new_cache = patched(copy, chosen, lengths, accepted)
    return attn_out, new_cache


def solution(mesh):
    return jax.shard_map(
        functools.partial(local, mesh.shape["seq"], mesh.shape["tp"]),
        mesh=mesh,
        in_specs=(
            P(None, "tp"),
            P(None, None, "seq", "tp"),
            P(None, "seq", "tp"),
            P("tp", "seq"),
            P(),
            P(),
            P(),
            P(),
        ),
        out_specs=(P("tp", "seq"), P(None, None, "seq", "tp")),
        check_vma=False,
    )
```

```python
import functools
import math

import jax
import jax.numpy as jnp
from jax import lax
from jax.experimental import pallas as pl
from jax.experimental.pallas import tpu as pltpu
from jax.sharding import PartitionSpec as P

HEAD = 128
Q = 64
ACC = 8
TENANTS = 4
GROUP = 8
DEAD = -1e30
FOLD = HEAD**-0.5 * math.log2(math.e)
WINDOW = 32
BF = jnp.bfloat16
F32 = jnp.float32
VMEM = pl.BlockSpec(memory_space=pltpu.VMEM)
SMEM = pl.BlockSpec(memory_space=pltpu.SMEM)
ANY = pl.BlockSpec(memory_space=pl.ANY)
HBM = pl.BlockSpec(memory_space=pltpu.HBM)
SMALL = pl.CostEstimate(flops=1, bytes_accessed=1, transcendentals=0)


def limit(mebibytes):
    return pltpu.CompilerParams(vmem_limit_bytes=mebibytes * 1024 * 1024)


def dot(a, b, contract=((1,), (0,))):
    return lax.dot_general(a, b, (contract, ((), ())), preferred_element_type=F32)


def live_devices(tenant, n_seq):
    return max(1, n_seq * 2**tenant // 8)


def live_chips(tenant, n_seq):
    return max(1, live_devices(tenant, n_seq) // 2)


def pieces(x):
    high = x.astype(BF).astype(F32)
    middle = (x - high).astype(BF).astype(F32)
    return high, middle, (x - high - middle).astype(BF).astype(F32)


def stat_tile(columns):
    rows = columns[0].shape[0]
    lane = lax.broadcasted_iota(jnp.int32, (rows, HEAD), 1)
    tile = jnp.zeros((rows, HEAD), F32)
    for h, column in enumerate(columns):
        for k, piece in enumerate(pieces(column)):
            tile = jnp.where(lane == k * GROUP + h, piece, tile)
    return tile.astype(BF)


def reach_kernel(parent_ref, out_ref):
    requests = parent_ref.shape[0]
    row_id = lax.broadcasted_iota(jnp.int32, (2 * Q, 2 * Q), 0)
    column_id = lax.broadcasted_iota(jnp.int32, (2 * Q, 2 * Q), 1)
    chains = []
    for r in range(0, requests, 2):
        up = []
        for k in range(2):
            parent = parent_ref[r + k : r + k + 1, :]
            up.append(jnp.where(parent < 0, -1, parent + k * Q))
        linked = (jnp.concatenate(up, axis=1) == row_id) | (row_id == column_id)
        chains.append(jnp.where(linked, 1.0, 0.0).astype(BF))
    doublings = (Q - 1).bit_length()
    for k in range(doublings):
        contract = ((0,), (1,)) if k == doublings - 1 else ((1,), (0,))
        chains = [jnp.minimum(dot(chain, chain, contract), 1.0).astype(BF) for chain in chains]
    for r in range(requests):
        k = r % 2 * Q
        out_ref[r] = chains[r // 2].astype(F32)[k : k + Q, k : k + Q]


def reach_of(parents):
    return pl.pallas_call(
        reach_kernel,
        out_shape=jax.ShapeDtypeStruct((parents.shape[0], Q, Q), F32),
        in_specs=[VMEM],
        out_specs=VMEM,
        compiler_params=limit(8),
        cost_estimate=SMALL,
        name="reach",
    )(parents)


def attend_kernel(tenant, owners, sources, n_sources, n_after, resident, *refs):
    len_ref, q_ref, kv_ref, reach_ref = refs[:4]
    drafts = refs[4 : 4 + n_sources]
    outs = refs[4 + n_sources + n_after :]
    mine, theirs, copy_ref, len_s, q_s, kv_s, draft_s, m_s, l_s, acc_s, load, store = outs
    count = draft_s.shape[0]
    span = kv_ref.shape[2]
    heads = q_ref.shape[1] // HEAD // 2
    half = heads * HEAD
    rows = heads * Q
    seq = lax.axis_index("seq")
    core = lax.rem(seq, 2)

    def loads(i):
        r = tenant + TENANTS * i
        if resident:
            return []
        return [
            pltpu.make_async_copy(q_ref.at[pl.ds(r * Q, Q), :], q_s.at[i], load.at[i, 0]),
            pltpu.make_async_copy(kv_ref.at[0, r], kv_s.at[i, 0], load.at[i, 1]),
            pltpu.make_async_copy(kv_ref.at[1, r], kv_s.at[i, 1], load.at[i, 2]),
        ]

    def stored(i):
        r = tenant + TENANTS * i
        return pltpu.make_async_copy(kv_ref.at[:, r] if resident else kv_s.at[i], copy_ref.at[:, r], store.at[i])

    def cached(i, x, columns):
        return kv_ref[x, tenant + TENANTS * i, :, columns] if resident else kv_s[i, x, :, columns]

    small = [pltpu.make_async_copy(len_ref, len_s, load.at[count, 0])]
    given = [pltpu.make_async_copy(drafts[sources[i]], draft_s.at[i], load.at[i, 3]) for i in range(count)]
    for copy in (*loads(0), *small, *[c for i in range(1, count) for c in loads(i)], *given):
        copy.start()
    for copy in small:
        copy.wait()

    def columns_of(g):
        kv = g * heads // GROUP
        return slice(kv * HEAD, (kv + 1) * HEAD)

    for i in range(count):
        r = tenant + TENANTS * i
        alive = len_s[r] - seq * span
        for copy in loads(i):
            copy.wait()
        given[i].wait()
        stored(i).start()

        def queries_of(g):
            held = q_ref.at[pl.ds(r * Q, Q)] if resident else q_s.at[i]
            return jnp.concatenate(
                [held[:, (g * heads + h) * HEAD : (g * heads + h + 1) * HEAD] for h in range(heads)], axis=0
            )

        @pl.when(alive > 0)
        def _():
            keep = lax.broadcasted_iota(jnp.int32, (span, HEAD), 0) < alive
            ones = jnp.where(keep, 1.0, 0.0).astype(BF)

            def scores(g):
                keys = cached(i, 0, columns_of(g))
                keys = jnp.where(keep, keys, jnp.broadcast_to(keys[:1], keys.shape))
                return dot(queries_of(g), keys, ((1,), (1,)))

            def weigh(g, m, w):
                values = cached(i, 1, columns_of(g))
                values = jnp.where(keep, values, jnp.zeros_like(values))
                o = dot(w, jnp.concatenate([values, ones], axis=1))
                place = slice(g * rows, (g + 1) * rows)
                m_s[place] = jnp.broadcast_to(m, (rows, HEAD))
                acc_s[place] = o[:, :HEAD]
                l_s[place] = o[:, HEAD:]

            upcoming = scores(0)
            pending = None
            for g in range(2):
                s = upcoming
                if g == 0:
                    upcoming = scores(1)
                m = jnp.max(s, axis=1, keepdims=True) * FOLD
                w = jnp.exp2(s * FOLD - m).astype(BF)
                if pending is not None:
                    weigh(*pending)
                pending = (g, m, w)
            weigh(*pending)

        @pl.when(alive <= 0)
        def _():
            m_s[...] = jnp.full_like(m_s, DEAD)
            l_s[...] = jnp.zeros_like(l_s)
            acc_s[...] = jnp.zeros_like(acc_s)

        @pl.when(seq == owners[i])
        def _():
            reach = jnp.concatenate([reach_ref[r]] * heads, axis=0) > 0.5
            for g in range(2):
                place = slice(g * rows, (g + 1) * rows)
                s = dot(queries_of(g), draft_s[i, 0, :, columns_of(g)], ((1,), (1,)))
                s = jnp.where(reach, s, DEAD)
                m_old = m_s[place]
                m = jnp.maximum(m_old, jnp.max(s, axis=1, keepdims=True) * FOLD)
                w = jnp.exp2(s * FOLD - m[:, :Q])
                shrink = jnp.exp2(m_old - m)
                l_s[place] = l_s[place] * shrink + jnp.sum(w, axis=1, keepdims=True)
                m_s[place] = m
                acc_s[place] = acc_s[place] * shrink + dot(w.astype(BF), draft_s[i, 1, :, columns_of(g)])

        def finish(g, out):
            stats = []
            for h in range(heads):
                place = slice((g * heads + h) * Q, (g * heads + h + 1) * Q)
                total = l_s[place]
                some = total > 0.0
                total = jnp.where(some, total, 1.0)
                out[i * Q : (i + 1) * Q, h * HEAD : (h + 1) * HEAD] = (acc_s[place] / total).astype(BF)
                stats.append(jnp.where(some, m_s[place] + jnp.log2(total), DEAD))
            out[i * Q : (i + 1) * Q, half:] = stat_tile(stats)

        for g in range(2):

            @pl.when(core == g)
            def _():
                finish(g, mine)
                finish(1 - g, theirs)

    for i in range(count):
        stored(i).wait()


def attend(tenant, queries, cache, reach, lengths, drafts, owners, sources, copy, after, resident=False):
    requests, span = cache.shape[1], cache.shape[2]
    count = requests // TENANTS
    used = sorted(set(sources))
    width, kv_width = queries.shape[1], cache.shape[3]
    wide = width // 2 + HEAD
    out = jax.ShapeDtypeStruct((count * Q, wide), BF)
    carried = [] if copy is None else [copy]
    extra = list(after) + carried
    return pl.pallas_call(
        functools.partial(attend_kernel, tenant, owners, [used.index(s) for s in sources], len(used), len(extra), resident),
        in_specs=[HBM] + [VMEM if resident else HBM] * 2 + [VMEM] + [HBM] * len(used) + [ANY] * len(extra),
        out_specs=[VMEM, VMEM, ANY],
        scratch_shapes=[
            pltpu.SMEM((requests,), jnp.int32),
            pltpu.VMEM((1 if resident else count, Q, width), BF),
            pltpu.VMEM((1, 1, 16, HEAD) if resident else (count, 2, span, kv_width), BF),
            pltpu.VMEM((count, 2, Q, kv_width), BF),
            pltpu.VMEM((Q * width // HEAD, HEAD), F32),
            pltpu.VMEM((Q * width // HEAD, HEAD), F32),
            pltpu.VMEM((Q * width // HEAD, HEAD), F32),
            pltpu.SemaphoreType.DMA((count + 1, 4)),
            pltpu.SemaphoreType.DMA((count,)),
        ],
        out_shape=[out, out, jax.ShapeDtypeStruct(cache.shape, BF)],
        input_output_aliases={3 + len(used) + len(extra): 2} if carried else {},
        compiler_params=limit(28),
        cost_estimate=SMALL,
        name=f"attend_{tenant}",
    )(lengths, queries, cache, reach, *[drafts[s] for s in used], *extra)


def combine_kernel(final, a_ref, b_ref, *rest):
    out_ref = rest[-1]
    rows = a_ref.shape[0]
    half = a_ref.shape[1] - HEAD
    heads = half // HEAD

    def stats_of(ref):
        tile = ref[:, half:].astype(F32)
        return tile[:, :GROUP] + tile[:, GROUP : 2 * GROUP] + tile[:, 2 * GROUP : 3 * GROUP]

    a, b = stats_of(a_ref), stats_of(b_ref)
    top = jnp.maximum(a, b)
    weight_a, weight_b = jnp.exp2(a - top), jnp.exp2(b - top)
    total = weight_a + weight_b
    weight_a, weight_b = weight_a / total, weight_b / total
    level = top + jnp.log2(total)
    for h in range(heads):
        place = slice(h * HEAD, (h + 1) * HEAD)
        out_ref[:, place] = (
            a_ref[:, place].astype(F32) * weight_a[:, h : h + 1]
            + b_ref[:, place].astype(F32) * weight_b[:, h : h + 1]
        ).astype(BF)
    if not final:
        out_ref[:, half:] = stat_tile(
            [jnp.broadcast_to(level[:, h : h + 1], (rows, HEAD)) for h in range(heads)]
        )


def combine(a, b, final, after=()):
    rows, wide = a.shape
    return pl.pallas_call(
        functools.partial(combine_kernel, final),
        out_shape=jax.ShapeDtypeStruct((rows, wide - HEAD if final else wide), BF),
        in_specs=[VMEM, VMEM] + [ANY for _ in after],
        out_specs=VMEM,
        compiler_params=limit(8),
        cost_estimate=SMALL,
        name="combine",
    )(a, b, *after)


def project_kernel(requests, n_tp, tenants, n_after, *refs):
    count = len(tenants)
    parts = refs[: 2 * count]
    w_ref = refs[2 * count]
    own_ref, *outs = refs[2 * count + 1 + n_after : -1]
    product = refs[-1]
    tp = lax.axis_index("tp")
    core = lax.rem(lax.axis_index("seq"), 2)
    half = w_ref.shape[0] // 2
    mine = jnp.concatenate([parts[2 * k][...] for k in range(count)], axis=0)
    other = jnp.concatenate([parts[2 * k + 1][...] for k in range(count)], axis=0)
    near = pl.ds(pl.multiple_of(core * half, half), half)
    far = pl.ds(pl.multiple_of((1 - core) * half, half), half)
    product[...] = dot(mine, w_ref[near, :]) + dot(other, w_ref[far, :])
    each = requests // TENANTS
    share = requests // n_tp
    taken = {}
    for k, tenant in enumerate(tenants):
        for i in range(each):
            r = tenant + TENANTS * i
            taken.setdefault(r // share, []).append((r % share, k * each + i))
    for owner in range(n_tp):
        for slot in range(n_tp):

            @pl.when((owner ^ tp) == slot)
            def _():
                for place, (_, block) in enumerate(sorted(taken[owner])):
                    value = product[block * Q : (block + 1) * Q, :]
                    target = own_ref if slot == 0 else outs[slot - 1]
                    target[place * Q : (place + 1) * Q, :] = value.astype(target.dtype)


def project(requests, n_tp, tenants, parts, weight, after):
    depth, columns = weight.shape
    rows = len(tenants) * (requests // TENANTS) * Q
    mine = rows // n_tp
    return pl.pallas_call(
        functools.partial(project_kernel, requests, n_tp, tenants, len(after)),
        in_specs=[VMEM] * (len(parts) + 1) + [ANY] * len(after),
        out_specs=[VMEM] * n_tp,
        out_shape=[jax.ShapeDtypeStruct((mine, columns), F32)]
        + [jax.ShapeDtypeStruct((mine, columns), BF)] * (n_tp - 1),
        scratch_shapes=[pltpu.VMEM((rows, columns), F32)],
        compiler_params=limit(20),
        cost_estimate=SMALL,
        name="project",
    )(*parts, weight, *after)


def pick_kernel(n_tokens, first, last, *refs):
    out_ref = refs[-1]
    value, *others = refs[: len(refs) - 1 - n_tokens]
    chip = lax.axis_index("seq") // 2
    inside = (chip >= first) & (chip <= last)

    @pl.when(inside)
    def _():
        out_ref[...] = value[...]

    @pl.when(jnp.logical_not(inside))
    def _():
        out_ref[...] = functools.reduce(jnp.add, [other[...] for other in others])


def pick(value, others, first, last, after):
    return pl.pallas_call(
        functools.partial(pick_kernel, len(after), first, last),
        out_shape=jax.ShapeDtypeStruct(value.shape, BF),
        in_specs=[VMEM] * (1 + len(others)) + [ANY] * len(after),
        out_specs=VMEM,
        compiler_params=limit(8),
        cost_estimate=SMALL,
        name="pick",
    )(value, *others, *after)


def stack_kernel(a_ref, b_ref, *rest):
    out_ref = rest[-1]
    size = a_ref.shape[0]
    out_ref[:size] = a_ref[...]
    out_ref[size:] = b_ref[...]


def stack(a, b, after):
    return pl.pallas_call(
        stack_kernel,
        out_shape=jax.ShapeDtypeStruct((2 * a.shape[0], *a.shape[1:]), BF),
        in_specs=[VMEM, VMEM] + [ANY] * len(after),
        out_specs=VMEM,
        compiler_params=limit(4),
        cost_estimate=SMALL,
        name="stack",
    )(a, b, *after)


def choose_kernel(path_ref, draft_ref, out_ref):
    seq = lax.axis_index("seq")
    row = lax.broadcasted_iota(jnp.int32, (ACC, Q), 0)
    column = lax.broadcasted_iota(jnp.int32, (ACC, Q), 1)
    picked = jnp.zeros((ACC, Q), jnp.int32)
    for j in range(ACC):
        picked = jnp.where(row == j, path_ref[seq, j], picked)
    selector = jnp.where(picked == column, 1.0, 0.0).astype(BF)
    for x in range(2):
        out_ref[0, x] = dot(selector, draft_ref[x]).astype(BF)


def choose(path, draft_kv):
    return pl.pallas_call(
        choose_kernel,
        out_shape=jax.ShapeDtypeStruct((1, 2, ACC, draft_kv.shape[2]), BF),
        in_specs=[SMEM, VMEM],
        out_specs=VMEM,
        compiler_params=limit(4),
        name="choose",
    )(path, draft_kv)


def patch_kernel(len_ref, accept_ref, cache_ref, chosen_ref, out_ref, window, load_sem, store_sem):
    requests, span = cache_ref.shape[1], cache_ref.shape[2]
    seq = lax.axis_index("seq")

    def place_of(r):
        first = len_ref[r] - seq * span
        start = jnp.clip(first // 16 * 16, 0, span - WINDOW)
        return first, pl.multiple_of(start, 16), (first + ACC > 0) & (first < span)

    def load(r):
        _, start, here = place_of(r)
        return here, pltpu.make_async_copy(
            cache_ref.at[:, r, pl.ds(start, WINDOW), :], window.at[r], load_sem.at[r]
        )

    def store(r):
        _, start, here = place_of(r)
        return here, pltpu.make_async_copy(
            window.at[r], out_ref.at[:, r, pl.ds(start, WINDOW), :], store_sem.at[r]
        )

    for r in range(requests):
        here, copy = load(r)
        pl.when(here)(copy.start)
    for r in range(requests):
        here, copy = load(r)
        first, start, _ = place_of(r)

        @pl.when(here)
        def _():
            copy.wait()
            row = lax.broadcasted_iota(jnp.int32, window.shape[2:], 0) + (start - first)
            for x in range(2):
                value = window[r, x].astype(F32)
                rows = chosen_ref[r ^ seq, x].astype(F32)
                for j in range(ACC):
                    value = jnp.where((row == j) & (j < accept_ref[r]), rows[j : j + 1], value)
                window[r, x] = value.astype(BF)
            store(r)[1].start()

    for r in range(requests):
        here, copy = store(r)
        pl.when(here)(copy.wait)


def patched(cache, chosen, lengths, accepted):
    requests = cache.shape[1]
    return pl.pallas_call(
        patch_kernel,
        out_shape=jax.ShapeDtypeStruct(cache.shape, BF),
        in_specs=[SMEM, SMEM, ANY, VMEM],
        out_specs=ANY,
        scratch_shapes=[
            pltpu.VMEM((requests, 2, WINDOW, cache.shape[3]), BF),
            pltpu.SemaphoreType.DMA((requests,)),
            pltpu.SemaphoreType.DMA((requests,)),
        ],
        input_output_aliases={2: 0},
        compiler_params=limit(8),
        name="patch_cache",
    )(lengths, accepted, cache, chosen)


def chip_pairs(pairs):
    return [(2 * a + c, 2 * b + c) for a, b in pairs for c in range(2)]


def local(n_seq, n_tp, queries, cache, draft_kv, out_weight, lengths, parents, path, accepted):
    requests = cache.shape[1]
    chips = n_seq // 2
    seq = lax.axis_index("seq")
    chip = seq // 2
    swap_pairs = [(s, s ^ 1) for s in range(n_seq)]

    def swap(array):
        return lax.ppermute(array, "seq", swap_pairs)

    def send(array, pairs):
        return lax.ppermute(array, "seq", chip_pairs(pairs))

    owners, sources, rounds = {}, {}, []
    for r in range(requests):
        owners[r] = r % live_devices(r % TENANTS, n_seq)
        sources[r] = 0
        if owners[r] != r:
            for k, taken in enumerate(rounds):
                if all(owners[r] != b for _, b in taken):
                    break
            else:
                k = len(rounds)
                rounds.append([])
            rounds[k].append((r, owners[r]))
            sources[r] = k + 1
    drafts = [draft_kv] + [lax.ppermute(draft_kv, "seq", pairs) for pairs in rounds]

    copy = None

    reach = reach_of(parents)

    def partial_of(tenant, after=()):
        nonlocal copy
        own = range(tenant, requests, TENANTS)
        mine, theirs, copy = attend(
            tenant,
            queries,
            cache,
            reach,
            lengths,
            drafts,
            [owners[r] for r in own],
            [sources[r] for r in own],
            copy,
            list(after),
            resident=tenant != 3,
        )
        return mine, swap(theirs)

    count = {tenant: live_chips(tenant, n_seq) for tenant in range(TENANTS)}
    steps, value = {}, {}
    for tenant in range(TENANTS):
        last, half = count[tenant] - 1, count[tenant] // 2
        steps[tenant] = [[(k, k + 1), (last - k, last - k - 1)] for k in range(half)]

    def join(tenant, pair, after=()):
        value[tenant] = combine(*pair, count[tenant] == 1, after)

    def advance(tenant, after=()):
        if steps[tenant]:
            arrived = send(value[tenant], steps[tenant].pop(0))
            value[tenant] = combine(value[tenant], arrived, not steps[tenant], after)

    def spread(tenant):
        first = max(count[tenant] // 2 - 1, 0)
        last = count[tenant] // 2
        top = (first, last)
        newest = value[tenant]
        if chips == 4 and last == 0:
            newest = early.get(tenant, None)
            if newest is None:
                newest = send(value[tenant], [(0, 2)])
            held = [newest, send(newest, [(2, 1)]), send(newest, [(2, 3)])]
        else:
            held = []
            while first > 0 or last < chips - 1:
                pairs = []
                if first > 0:
                    pairs.append((first, first - 1))
                    first -= 1
                if last < chips - 1:
                    pairs.append((last, last + 1))
                    last += 1
                newest = send(newest, pairs)
                held.append(newest)
        return held, top

    def settle(tenant, held, top, after):
        if held:
            value[tenant] = pick(value[tenant], held, top[0], top[1], after)
        whole[tenant] = (value[tenant], swap(value[tenant]))

    chosen = choose(path, draft_kv)

    def gather(after):
        nonlocal chosen
        if chosen.shape[0] < n_seq:
            pairs = [(s, s ^ chosen.shape[0]) for s in range(n_seq)]
            chosen = stack(chosen, lax.ppermute(chosen, "seq", pairs), after)

    early = {}
    join(3, partial_of(3))
    zero = partial_of(0, [value[3]])
    advance(3, [zero[0]])
    join(0, zero, [value[3]])
    gather([value[0]])
    two = partial_of(2, [value[0], chosen])
    join(2, two)
    gather([value[2]])
    if chips == 4:
        early[0] = send(value[0], [(0, 2)])
    one = partial_of(1, [value[2], chosen] + list(early.values()))
    advance(3, [one[0]])
    advance(2, [value[3]])
    join(1, one, [value[2]])
    whole = {}
    for tenant in (3, 0, 2, 1):
        while steps[tenant]:
            advance(tenant, [value[1]])

    def sums(tenants, after):
        parts = [part for tenant in tenants for part in whole[tenant]]
        own, *others = project(requests, n_tp, tenants, parts, out_weight, after)
        arrived = [
            lax.ppermute(other, "tp", [(t, t ^ (k + 1)) for t in range(n_tp)]).astype(F32)
            for k, other in enumerate(others)
        ]
        return own, functools.reduce(jnp.add, arrived, own).astype(BF)

    moves = {tenant: spread(tenant) for tenant in (2, 1, 0, 3)}
    first_hop = moves[2][0][:1]
    settle(0, *moves[0], first_hop)
    settle(3, *moves[3], [value[0]])
    own, one_sum = sums((3, 0), [])
    settle(1, *moves[1], [own])
    settle(2, *moves[2], [own])
    _, other_sum = sums((2, 1), [one_sum])

    assert requests == 2 * n_tp
    even = lax.axis_index("tp") % 2 == 0
    attn_out = jnp.concatenate(
        [jnp.where(even, one_sum, other_sum), jnp.where(even, other_sum, one_sum)], axis=0
    )

    while chosen.shape[0] < n_seq:
        gather([value[1]])
    new_cache = patched(copy, chosen, lengths, accepted)
    return attn_out, new_cache


def solution(mesh):
    return jax.shard_map(
        functools.partial(local, mesh.shape["seq"], mesh.shape["tp"]),
        mesh=mesh,
        in_specs=(
            P(None, "tp"),
            P(None, None, "seq", "tp"),
            P(None, "seq", "tp"),
            P("tp", "seq"),
            P(),
            P(),
            P(),
            P(),
        ),
        out_specs=(P("tp", "seq"), P(None, None, "seq", "tp")),
        check_vma=False,
    )
```
